128 devices in a mesh: img: 16 (over y_hi, x, core), phr: 8 (over y_lo, z).
Axes of the slice: x: 4, y: 4 (y_hi: 2, y_lo: 2; y = y_hi * 2 + y_lo), z: 4, core: 2. Of those that a mesh axis runs over, the one named last changes fastest.
Arguments:
- regions: bfloat16 [16384, 1024], P('img'), may hold values from -3 to 3
- phrases: bfloat16 [32768, 1024], P('phr'), may hold values from -6 to 6
- positive: int32 [16384], P('img'), may hold values from 0 to 32767
- valid: int32 [512, 32], P('img'), may hold values 0 or 1
Outputs:
- grad_regions: bfloat16 [16384, 1024], P('img', 'phr')
- grad_phrases: bfloat16 [32768, 1024], P(('phr', 'img'))
The draws below stay inside these ranges and needn't reach their ends.
All inputs are finite; a program needn't handle non-finite values. No bound on the sum of `valid` on one device may be relied on, other than what follows from the above.
Results may differ from the reference program's by a relative error of at most 0.0034.
Values may be sent and summed in bfloat16 or wider, within the bound.
No kernel may reach another device: no remote copies, remote signals or barrier semaphores. Data moves between devices by JAX's collectives and lax.ppermute only.
A program may use at most 128 MiB of HBM per device.

```python
import jax
import jax.numpy as jnp
from jax import lax

D = 1024
BOXES = 32
NIMG = 512
NREG = 16384
NPHR = 32768


def shared_phrases(key):
    return jnp.clip(jax.random.normal(key, (NPHR, D), jnp.float32), -6.0, 6.0)


def draw_phrases(key, part):
    table = shared_phrases(key)
    return table.astype(jnp.bfloat16)


def draw_regions(key, part):
    key = jax.random.fold_in(key, 5)
    first_key = jax.random.fold_in(key, 0)
    base = jnp.clip(jax.random.normal(first_key, (NREG, D), jnp.float32), -6.0, 6.0) / 32.0
    return base.astype(jnp.bfloat16)


def with_ends(result, own_key, least, top_value):
    dims = result.shape
    index_at = [jax.random.randint(jax.random.fold_in(own_key, axis), (), 0, dims[axis]) for axis in range(len(dims))]
    result = result.at[tuple(index_at)].set(least)
    longest = dims.index(max(dims))
    index_at[longest] = (index_at[longest] + 1) % dims[longest]
    return result.at[tuple(index_at)].set(top_value)


def setup_inputs(seed: int = 0) -> dict:
    keys = jax.random.split(jax.random.key(seed), 5)
    return {
        "regions": draw_regions(jax.random.fold_in(keys[4], 71), 0),
        "phrases": draw_phrases(jax.random.fold_in(keys[4], 71), 0),
        "positive": with_ends(jax.random.randint(keys[2], (NREG,), 0, NPHR), jax.random.fold_in(keys[2], 1), 0, NPHR - 1).astype(jnp.int32),
        "valid": with_ends((jax.random.randint(keys[3], (NIMG, BOXES), 0, 4) < 3).astype(jnp.int32), jax.random.fold_in(keys[3], 1), 0, 1),
    }


logit_scale = 2.0


def reference(regions, phrases, positive, valid):
    weight = valid.reshape(-1).astype(jnp.float32)
    block = 512
    count = NREG // block
    region_blocks = regions.reshape(count, block, D)
    positive_blocks = positive.reshape(count, block)
    weight_blocks = weight.reshape(count, block)
    columns = jnp.arange(NPHR, dtype=jnp.int32)

    def step(carry, items):
        rows, target, scale = items
        scores = logit_scale * lax.dot_general(rows, phrases, (((1,), (1,)), ((), ())), preferred_element_type=jnp.float32)
        top = jnp.max(scores, axis=1)
        total = jnp.sum(jnp.exp(scores - top[:, None]), axis=1)
        lse = top + jnp.log(total)
        hits = (target[:, None] == columns[None, :]).astype(jnp.float32)
        coeff = (scale[:, None] * (jnp.exp(scores - lse[:, None]) - hits)).astype(jnp.bfloat16)
        grad_rows = (logit_scale * jnp.dot(coeff, phrases, preferred_element_type=jnp.float32)).astype(jnp.bfloat16)
        carry = carry + logit_scale * lax.dot_general(coeff, rows, (((0,), (0,)), ((), ())), preferred_element_type=jnp.float32)
        return carry, grad_rows

    start = jnp.zeros((NPHR, D), jnp.float32)
    grad_phr, grad_reg = lax.scan(step, start, (region_blocks, positive_blocks, weight_blocks))
    return grad_reg.reshape(NREG, D), grad_phr.astype(jnp.bfloat16)
```

```python
import math

import jax
import jax.numpy as jnp
from jax import lax
from jax.experimental import pallas as pl
from jax.experimental.pallas import tpu as pltpu
from jax.sharding import PartitionSpec as P

logit_scale = 2.0
log2e = math.log2(math.e)
BLK = 256
ORDER = (2, 1, 3, 0)
VMEM = 48 * 1024 * 1024


def img_perm(f):
    pairs = []
    for y in range(2):
        for x in range(4):
            for c in range(2):
                y2, x2, c2 = f(y, x, c)
                pairs.append(((y * 4 + x) * 2 + c, (y2 * 4 + x2) * 2 + c2))
    return pairs


def phr_perm(f):
    pairs = []
    for y in range(2):
        for z in range(4):
            y2, z2 = f(y, z)
            pairs.append((y * 4 + z, y2 * 4 + z2))
    return pairs


CORE = img_perm(lambda y, x, c: (y, x, 1 - c))
X1 = img_perm(lambda y, x, c: (y, x ^ 1, c))
X3 = img_perm(lambda y, x, c: (y, x ^ 3, c))
YH = img_perm(lambda y, x, c: (1 - y, x, c))


def over_img(a, perm):
    return lax.ppermute(a, "img", perm)


def over_phr(a, dy, dz):
    return lax.ppermute(a, "phr", phr_perm(lambda y, z: (y ^ dy, z ^ dz)))


def scores_kernel(blk, p_ref, r_ref, e_ref, m_ref, l_ref):
    s = lax.dot_general(
        p_ref[...], r_ref[...], (((1,), (1,)), ((), ())), preferred_element_type=jnp.float32
    )
    s = s * (logit_scale * log2e)
    m = jnp.max(s, axis=0, keepdims=True)
    e = jnp.exp2(s - m)
    e_ref[...] = e
    m_ref[0] = m
    l_ref[0] = jnp.sum(e, axis=0, keepdims=True)


def scores_call(blk, phrases, regions):
    rows, dim = regions.shape
    tiles = phrases.shape[0] // BLK // 2
    return pl.pallas_call(
        scores_kernel,
        grid_spec=pltpu.PrefetchScalarGridSpec(
            num_scalar_prefetch=1,
            grid=(tiles,),
            in_specs=[
                pl.BlockSpec((BLK, dim), lambda j, blk: (blk[j], 0)),
                pl.BlockSpec((rows, dim), lambda j, blk: (0, 0)),
            ],
            out_specs=[
                pl.BlockSpec((BLK, rows), lambda j, blk: (j, 0)),
                pl.BlockSpec((1, 1, rows), lambda j, blk: (j, 0, 0)),
                pl.BlockSpec((1, 1, rows), lambda j, blk: (j, 0, 0)),
            ],
        ),
        out_shape=[
            jax.ShapeDtypeStruct((tiles * BLK, rows), jnp.float32),
            jax.ShapeDtypeStruct((tiles, 1, rows), jnp.float32),
            jax.ShapeDtypeStruct((tiles, 1, rows), jnp.float32),
        ],
        compiler_params=pltpu.CompilerParams(vmem_limit_bytes=VMEM),
        cost_estimate=pl.CostEstimate(
            flops=2 * tiles * BLK * rows * dim,
            bytes_accessed=tiles * BLK * rows * 4 + rows * dim * 2 + tiles * BLK * dim * 2,
            transcendentals=tiles * BLK * rows,
        ),
        name="scores",
    )(blk, phrases, regions)


def coefficients(e, scale, pos, first):
    column = first + lax.broadcasted_iota(jnp.int32, e.shape, 0)
    return (e * scale - (column == pos).astype(jnp.float32)).astype(jnp.bfloat16)


def phrase_kernel(
    base, off, eo, ep, so, sp, po, pp, ro, rp, send_a, send_b, keep_a, keep_b
):
    i = pl.program_id(0)
    first = off[base + i]
    half = ro.shape[1] // 2
    co = coefficients(eo[...], so[0], po[...], first)
    cp = coefficients(ep[...], sp[0], pp[...], first)
    acc = jnp.dot(co, ro[...], preferred_element_type=jnp.float32)
    acc += jnp.dot(cp, rp[...], preferred_element_type=jnp.float32)
    acc = logit_scale * acc
    left, right = acc[:, :half], acc[:, half:]
    places = (
        (send_a, 1, send_b, 1),
        (send_a, 0, keep_b, 1),
        (keep_a, 1, send_b, 0),
        (keep_a, 0, keep_b, 0),
    )
    for step, (a, ia, b, ib) in enumerate(places):

        @pl.when(i == step)
        def _():
            a[ia] = left.astype(a.dtype)
            b[ib] = right.astype(b.dtype)


def phrase_call(base, off, eo, ep, so, sp, po, pp, ro, rp):
    rows, dim = ro.shape
    half = dim // 2
    e_spec = pl.BlockSpec((BLK, rows), lambda i, off: (base + i, 0))
    s_spec = pl.BlockSpec((1, 1, rows), lambda i, off: (base + i, 0, 0))
    p_spec = pl.BlockSpec((1, rows), lambda i, off: (0, 0))
    r_spec = pl.BlockSpec((rows, dim), lambda i, off: (0, 0))
    out_spec = pl.BlockSpec((2, BLK, half), lambda i, off: (0, 0, 0))
    return pl.pallas_call(
        lambda *refs: phrase_kernel(base, *refs),
        grid_spec=pltpu.PrefetchScalarGridSpec(
            num_scalar_prefetch=1,
            grid=(4,),
            in_specs=[e_spec, e_spec, s_spec, s_spec, p_spec, p_spec, r_spec, r_spec],
            out_specs=[out_spec] * 4,
        ),
        out_shape=[jax.ShapeDtypeStruct((2, BLK, half), jnp.bfloat16)] * 2
        + [jax.ShapeDtypeStruct((2, BLK, half), jnp.float32)] * 2,
        compiler_params=pltpu.CompilerParams(vmem_limit_bytes=VMEM),
        cost_estimate=pl.CostEstimate(
            flops=2 * 4 * BLK * 2 * rows * dim,
            bytes_accessed=4 * BLK * 2 * rows * 4 + 2 * rows * dim * 2 + 4 * BLK * dim * 3,
            transcendentals=0,
        ),
        name="phrase_part",
    )(off, eo, ep, so, sp, po, pp, ro, rp)


def region_kernel(blk, off, dst, p_hbm, e, s, pos, out, p_buf, coeff, acc, sem):
    tiles = s.shape[0]

    @pl.when(pl.program_id(0) == 0)
    def _():
        copies = [
            pltpu.make_async_copy(
                p_hbm.at[pl.ds(pl.multiple_of(blk[j] * BLK, BLK), BLK)],
                p_buf.at[pl.ds(j * BLK, BLK)],
                sem.at[j],
            )
            for j in range(tiles)
        ]
        for copy in copies:
            copy.start()
        for copy in copies:
            copy.wait()

    for j in range(tiles):
        part = pl.ds(j * BLK, BLK)
        coeff[part] = coefficients(e[part], s[j], pos[...], off[j])
    acc[...] = logit_scale * lax.dot_general(
        coeff[...], p_buf[...], (((0,), (0,)), ((), ())), preferred_element_type=jnp.float32
    )
    for k in range(8):
        cols = pl.ds(pl.multiple_of(dst[k] * 128, 128), 128)
        out[k] = acc[:, cols].astype(out.dtype)


def region_call(blk, off, dst, phrases, e, s, pos, dtype):
    tiles, _, rows = s.shape
    dim = phrases.shape[1]
    return pl.pallas_call(
        region_kernel,
        grid_spec=pltpu.PrefetchScalarGridSpec(
            num_scalar_prefetch=3,
            grid=(rows // BLK,),
            in_specs=[
                pl.BlockSpec(memory_space=pl.ANY),
                pl.BlockSpec((tiles * BLK, BLK), lambda i, *_: (0, i)),
                pl.BlockSpec((tiles, 1, BLK), lambda i, *_: (0, 0, i)),
                pl.BlockSpec((1, BLK), lambda i, *_: (0, i)),
            ],
            out_specs=pl.BlockSpec((8, BLK, 128), lambda i, *_: (0, i, 0)),
            scratch_shapes=[
                pltpu.VMEM((tiles * BLK, dim), jnp.bfloat16),
                pltpu.VMEM((tiles * BLK, BLK), jnp.bfloat16),
                pltpu.VMEM((BLK, dim), jnp.float32),
                pltpu.SemaphoreType.DMA((tiles,)),
            ],
        ),
        out_shape=jax.ShapeDtypeStruct((8, rows, 128), dtype),
        compiler_params=pltpu.CompilerParams(vmem_limit_bytes=VMEM),
        cost_estimate=pl.CostEstimate(
            flops=2 * tiles * BLK * rows * dim,
            bytes_accessed=tiles * BLK * rows * 4 + rows * dim * 4 + tiles * BLK * dim * 2,
            transcendentals=0,
        ),
        name="region_part",
    )(blk, off, dst, phrases, e, s, pos)


def combine(first, *others):
    top = first[0]
    for other in others:
        top = jnp.maximum(top, other[0])
    total = first[1] * jnp.exp2(first[0] - top)
    for other in others:
        total += other[1] * jnp.exp2(other[0] - top)
    return jnp.stack([top, total])


def per_device(regions, phrases, positive, valid):
    img, phr = lax.axis_index("img"), lax.axis_index("phr")
    core, x, yh = img % 2, (img // 2) % 4, img // 8
    yl, z = phr // 4, phr % 4
    blk = jnp.stack([((yh ^ e) * 4 + (x ^ d)) * 2 + core for e in (1, 0) for d in ORDER])
    off = phr * phrases.shape[0] + blk * BLK
    dst = jnp.stack([(yl ^ dy) * 4 + (z ^ dz) for dy in (0, 1) for dz in range(4)])
    blk, off, dst = (a.astype(jnp.int32) for a in (blk, off, dst))

    pos_own = jnp.where(valid.reshape(-1) != 0, positive, -1)
    regions_pair = over_img(regions, CORE)
    pos_pair = over_img(pos_own, CORE)
    e_own, m_own, l_own = scores_call(blk, phrases, regions)
    e_pair, m_pair, l_pair = scores_call(blk, phrases, regions_pair)

    m = jnp.stack([m_own[:, 0], m_pair[:, 0]])
    l = jnp.stack([l_own[:, 0], l_pair[:, 0]])
    top = jnp.max(m, axis=1)
    state = jnp.stack([top, jnp.sum(l * jnp.exp2(m - top[:, None]), axis=1)])
    state = combine(state, over_img(state, CORE)[:, ::-1])
    state = combine(state, over_phr(state, 1, 0))
    state = combine(state, *[over_phr(state, 0, dz) for dz in (1, 2, 3)])
    lse = state[0] + jnp.log2(state[1])
    s_own = jnp.where(pos_own >= 0, jnp.exp2(m_own - lse[0]), 0.0)
    s_pair = jnp.where(pos_pair >= 0, jnp.exp2(m_pair - lse[1]), 0.0)
    po, pp = pos_own[None], pos_pair[None]

    totals = []
    for base in (0, 4):
        send_a, send_b, keep_a, keep_b = phrase_call(
            base, off, e_own, e_pair, s_own, s_pair, po, pp, regions, regions_pair
        )
        got_a = over_img(send_a, X1)
        got_b = over_img(send_b, X3)
        sum_a = keep_a + got_a.astype(jnp.float32)
        sum_b = keep_b + got_b.astype(jnp.float32)
        last_a = over_img(sum_a[1].astype(jnp.bfloat16), X3)
        last_b = over_img(sum_b[1].astype(jnp.bfloat16), X1)
        totals.append(
            jnp.concatenate(
                [sum_a[0] + last_a.astype(jnp.float32), sum_b[0] + last_b.astype(jnp.float32)],
                axis=1,
            )
        )
    far, near = totals
    grad_phrases = near + over_img(far.astype(jnp.bfloat16), YH).astype(jnp.float32)

    for_pair = region_call(blk, off, dst, phrases, e_pair, s_pair, pp, jnp.bfloat16)
    from_pair = over_img(for_pair, CORE)
    kept = region_call(blk, off, dst, phrases, e_own, s_own, po, jnp.float32)
    kept = kept + from_pair.astype(jnp.float32)
    sends = kept[1:].astype(jnp.bfloat16)
    grad_regions = kept[0]
    for k in range(1, 8):
        grad_regions += over_phr(sends[k - 1], k // 4, k % 4).astype(jnp.float32)
    return grad_regions.astype(jnp.bfloat16), grad_phrases.astype(jnp.bfloat16)


def solution(mesh):
    in_specs = (P("img", None), P("phr", None), P("img"), P("img", None))
    out_specs = (P("img", "phr"), P(("phr", "img"), None))
    return jax.shard_map(
        per_device, mesh=mesh, in_specs=in_specs, out_specs=out_specs, check_vma=False
    )
```

```python
import math

import jax
import jax.numpy as jnp
from jax import lax
from jax.experimental import pallas as pl
from jax.experimental.pallas import tpu as pltpu
from jax.sharding import PartitionSpec as P

logit_scale = 2.0
log2e = math.log2(math.e)
BLK = 256
ORDER = (2, 1, 3, 0)
VMEM = 8 * 1024 * 1024


def img_perm(f):
    pairs = []
    for y in range(2):
        for x in range(4):
            for c in range(2):
                y2, x2, c2 = f(y, x, c)
                pairs.append(((y * 4 + x) * 2 + c, (y2 * 4 + x2) * 2 + c2))
    return pairs


def phr_perm(f):
    pairs = []
    for y in range(2):
        for z in range(4):
            y2, z2 = f(y, z)
            pairs.append((y * 4 + z, y2 * 4 + z2))
    return pairs


CORE = img_perm(lambda y, x, c: (y, x, 1 - c))
X1 = img_perm(lambda y, x, c: (y, x ^ 1, c))
X3 = img_perm(lambda y, x, c: (y, x ^ 3, c))
YH = img_perm(lambda y, x, c: (1 - y, x, c))


def over_img(a, perm):
    return lax.ppermute(a, "img", perm)


def over_phr(a, dy, dz):
    return lax.ppermute(a, "phr", phr_perm(lambda y, z: (y ^ dy, z ^ dz)))


def vmem(a):
    return pltpu.with_memory_space_constraint(a, pltpu.VMEM)


WHOLE = pl.BlockSpec(memory_space=pltpu.VMEM)
SCALAR = pl.BlockSpec(memory_space=pltpu.SMEM)
HBM = pl.BlockSpec(memory_space=pltpu.HBM)


def call(body, in_specs, outs, name, flops, **kwargs):
    return pl.pallas_call(
        body,
        in_specs=in_specs,
        out_specs=[WHOLE] * len(outs),
        out_shape=[pltpu.VMEM(*out) for out in outs],
        compiler_params=pltpu.CompilerParams(vmem_limit_bytes=VMEM),
        cost_estimate=pl.CostEstimate(flops=flops, bytes_accessed=1 << 20, transcendentals=0),
        name=name,
        **kwargs,
    )


def score_block(j, phrases, regions, e, m, l):
    part = pl.ds(j * BLK, BLK)
    s = lax.dot_general(
        phrases[part], regions[...], (((1,), (1,)), ((), ())), preferred_element_type=jnp.float32
    )
    s = s * (logit_scale * log2e)
    top = jnp.max(s, axis=0, keepdims=True)
    value = jnp.exp2(s - top)
    e[part] = value
    m[j] = top
    l[j] = jnp.sum(value, axis=0, keepdims=True)


def first_scores_kernel(blk, p_hbm, r_hbm, e, m, l, phrases, regions, sem):
    tiles = m.shape[0]
    copies = [pltpu.make_async_copy(r_hbm, regions, sem.at[tiles])]
    for j in range(tiles):
        rows = pl.ds(pl.multiple_of(blk[j] * BLK, BLK), BLK)
        copies.append(
            pltpu.make_async_copy(p_hbm.at[rows], phrases.at[pl.ds(j * BLK, BLK)], sem.at[j])
        )
    for copy in copies:
        copy.start()
    copies[0].wait()
    for j in range(tiles):
        copies[j + 1].wait()
        score_block(j, phrases, regions, e, m, l)


def first_scores_call(blk, phrases, regions):
    rows, dim = regions.shape
    half = phrases.shape[0] // 2
    tiles = half // BLK
    return call(
        first_scores_kernel,
        [SCALAR, HBM, HBM],
        [
            ((half, rows), jnp.float32),
            ((tiles, 1, rows), jnp.float32),
            ((tiles, 1, rows), jnp.float32),
            ((half, dim), phrases.dtype),
            ((rows, dim), regions.dtype),
        ],
        "first_scores",
        2 * half * rows * dim,
        scratch_shapes=[pltpu.SemaphoreType.DMA((tiles + 1,))],
    )(blk, *[pltpu.with_memory_space_constraint(a, pltpu.HBM) for a in (phrases, regions)])


def scores_kernel(phrases, regions, e, m, l):
    for j in range(m.shape[0]):
        score_block(j, phrases, regions, e, m, l)


def scores_call(phrases, regions):
    rows, dim = regions.shape
    half = phrases.shape[0]
    tiles = half // BLK
    return call(
        scores_kernel,
        [WHOLE] * 2,
        [
            ((half, rows), jnp.float32),
            ((tiles, 1, rows), jnp.float32),
            ((tiles, 1, rows), jnp.float32),
        ],
        "scores",
        2 * half * rows * dim,
    )(vmem(phrases), vmem(regions))


def coefficients(e, scale, pos, first):
    column = first + lax.broadcasted_iota(jnp.int32, e.shape, 0)
    return (e * scale - (column == pos).astype(jnp.float32)).astype(jnp.bfloat16)


def phrase_kernel(base, off, eo, ep, so, sp, po, pp, ro, rp, send_a, send_b, keep_a, keep_b):
    half = ro.shape[1] // 2
    places = (
        (send_a, 1, send_b, 1),
        (send_a, 0, keep_b, 1),
        (keep_a, 1, send_b, 0),
        (keep_a, 0, keep_b, 0),
    )
    for step, (a, ia, b, ib) in enumerate(places):
        j = base + step
        part = pl.ds(j * BLK, BLK)
        co = coefficients(eo[part], so[j], po[...], off[j])
        cp = coefficients(ep[part], sp[j], pp[...], off[j])
        acc = jnp.dot(co, ro[...], preferred_element_type=jnp.float32)
        acc += jnp.dot(cp, rp[...], preferred_element_type=jnp.float32)
        acc = logit_scale * acc
        a[ia] = acc[:, :half].astype(a.dtype)
        b[ib] = acc[:, half:].astype(b.dtype)


def phrase_call(base, off, *arrays):
    rows, dim = arrays[-1].shape
    shape = (2, BLK, dim // 2)
    return call(
        lambda *refs: phrase_kernel(base, *refs),
        [SCALAR] + [WHOLE] * len(arrays),
        [(shape, jnp.bfloat16)] * 2 + [(shape, jnp.float32)] * 2,
        "phrase_part",
        2 * 4 * BLK * 2 * rows * dim,
    )(off, *[vmem(a) for a in arrays])


def region_kernel(phr, off, e, s, pos, phrases, out):
    tiles, _, rows = s.shape
    for i in range(0, rows, BLK):
        lanes = pl.ds(i, BLK)
        coeff = jnp.concatenate(
            [
                coefficients(e[pl.ds(j * BLK, BLK), lanes], s[j, :, lanes], pos[:, lanes], off[j])
                for j in range(tiles)
            ],
            axis=0,
        )
        acc = logit_scale * lax.dot_general(
            coeff, phrases[...], (((0,), (0,)), ((), ())), preferred_element_type=jnp.float32
        )
        for q in range(8):
            out[phr[0] ^ q, lanes] = acc[:, q * 128 : (q + 1) * 128].astype(out.dtype)


def region_call(phr, off, e, s, pos, phrases, dtype):
    tiles, _, rows = s.shape
    dim = phrases.shape[1]
    arrays = (e, s, pos, phrases)
    return call(
        region_kernel,
        [SCALAR] * 2 + [WHOLE] * len(arrays),
        [((8, rows, 128), dtype)],
        "region_part",
        2 * tiles * BLK * rows * dim,
    )(phr, off, *[vmem(a) for a in arrays])[0]


GROUPS = [[(i * 2 + c) * 8 + p for c in range(2) for p in range(8)] for i in range(8)]


def per_device(regions, phrases, positive, valid):
    img, phr = lax.axis_index("img"), lax.axis_index("phr")
    core = img % 2
    blk = jnp.stack([img ^ (e * 8 + d * 2) for e in (1, 0) for d in ORDER]).astype(jnp.int32)
    off = (phr * phrases.shape[0] + blk * BLK).astype(jnp.int32)
    phr_id = phr.astype(jnp.int32)[None]

    pos_own = jnp.where(valid.reshape(-1) != 0, positive, -1)
    regions_pair = over_img(regions, CORE)
    pos_pair = over_img(pos_own, CORE)
    e_own, m_own, l_own, phrases, regions = first_scores_call(blk, phrases, regions)
    e_pair, m_pair, l_pair = scores_call(phrases, regions_pair)

    m = jnp.stack([m_own[:, 0], m_pair[:, 0]])
    l = jnp.stack([l_own[:, 0], l_pair[:, 0]])
    top = jnp.max(m, axis=1)
    state = jnp.stack([top, jnp.sum(l * jnp.exp2(m - top[:, None]), axis=1)])
    to_core = jnp.arange(2, dtype=jnp.int32)[:, None, None, None, None]
    sends = jnp.where(to_core == core, state, state[:, ::-1])
    sends = jnp.broadcast_to(sends, (2, 8) + state.shape).reshape((16,) + state.shape)
    got = lax.all_to_all(
        sends, ("img", "phr"), 0, 0, tiled=True, axis_index_groups=GROUPS
    )
    top = jnp.max(got[:, 0], axis=0)
    lse = top + jnp.log2(jnp.sum(got[:, 1] * jnp.exp2(got[:, 0] - top), axis=0))
    s_own = jnp.where(pos_own >= 0, jnp.exp2(m_own - lse[0]), 0.0)
    s_pair = jnp.where(pos_pair >= 0, jnp.exp2(m_pair - lse[1]), 0.0)
    po, pp = pos_own[None], pos_pair[None]

    totals = []
    for base in (0, 4):
        send_a, send_b, keep_a, keep_b = phrase_call(
            base, off, e_own, e_pair, s_own, s_pair, po, pp, regions, regions_pair
        )
        got_a = over_img(send_a, X1)
        got_b = over_img(send_b, X3)
        sum_a = keep_a + got_a.astype(jnp.float32)
        sum_b = keep_b + got_b.astype(jnp.float32)
        last_a = over_img(sum_a[1].astype(jnp.bfloat16), X3)
        last_b = over_img(sum_b[1].astype(jnp.bfloat16), X1)
        totals.append(
            jnp.concatenate(
                [sum_a[0] + last_a.astype(jnp.float32), sum_b[0] + last_b.astype(jnp.float32)],
                axis=1,
            )
        )
    far, near = totals
    grad_phrases = near + over_img(far.astype(jnp.bfloat16), YH).astype(jnp.float32)

    for_pair = region_call(phr_id, off, e_pair, s_pair, pp, phrases, jnp.bfloat16)
    from_pair = over_img(for_pair, CORE)
    kept = region_call(phr_id, off, e_own, s_own, po, phrases, jnp.float32)
    kept = kept + from_pair.astype(jnp.float32)
    sends = kept[1:].astype(jnp.bfloat16)
    grad_regions = kept[0]
    for k in range(1, 8):
        grad_regions += over_phr(sends[k - 1], k // 4, k % 4).astype(jnp.float32)
    return grad_regions.astype(jnp.bfloat16), grad_phrases.astype(jnp.bfloat16)


def solution(mesh):
    in_specs = (P("img", None), P("phr", None), P("img"), P("img", None))
    out_specs = (P("img", "phr"), P(("phr", "img"), None))
    return jax.shard_map(
        per_device, mesh=mesh, in_specs=in_specs, out_specs=out_specs, check_vma=False
    )
```

```python
import math

import jax
import jax.numpy as jnp
from jax import lax
from jax.experimental import pallas as pl
from jax.experimental.pallas import tpu as pltpu
from jax.sharding import PartitionSpec as P

logit_scale = 2.0
log2e = math.log2(math.e)
BLK = 256
ORDER = (2, 1, 3, 0)
VMEM = 8 * 1024 * 1024


def img_perm(f):
    pairs = []
    for y in range(2):
        for x in range(4):
            for c in range(2):
                y2, x2, c2 = f(y, x, c)
                pairs.append(((y * 4 + x) * 2 + c, (y2 * 4 + x2) * 2 + c2))
    return pairs


def phr_perm(f):
    pairs = []
    for y in range(2):
        for z in range(4):
            y2, z2 = f(y, z)
            pairs.append((y * 4 + z, y2 * 4 + z2))
    return pairs


CORE = img_perm(lambda y, x, c: (y, x, 1 - c))
X1 = img_perm(lambda y, x, c: (y, x ^ 1, c))
X3 = img_perm(lambda y, x, c: (y, x ^ 3, c))
YH = img_perm(lambda y, x, c: (1 - y, x, c))


def over_img(a, perm):
    return lax.ppermute(a, "img", perm)


def over_phr(a, dy, dz):
    return lax.ppermute(a, "phr", phr_perm(lambda y, z: (y ^ dy, z ^ dz)))


def vmem(a):
    return pltpu.with_memory_space_constraint(a, pltpu.VMEM)


WHOLE = pl.BlockSpec(memory_space=pltpu.VMEM)
SCALAR = pl.BlockSpec(memory_space=pltpu.SMEM)
HBM = pl.BlockSpec(memory_space=pltpu.HBM)


def call(body, in_specs, outs, name, **kwargs):
    return pl.pallas_call(
        body,
        in_specs=in_specs,
        out_specs=[WHOLE] * len(outs),
        out_shape=[pltpu.VMEM(*out) for out in outs],
        compiler_params=pltpu.CompilerParams(vmem_limit_bytes=VMEM),
        cost_estimate=pl.CostEstimate(flops=1, bytes_accessed=1, transcendentals=0),
        name=name,
        **kwargs,
    )


def score_block(j, phrases, regions, e, m, l):
    part = pl.ds(j * BLK, BLK)
    s = lax.dot_general(
        phrases[part], regions[...], (((1,), (1,)), ((), ())), preferred_element_type=jnp.float32
    )
    s = s * (logit_scale * log2e)
    top = jnp.max(s, axis=0, keepdims=True)
    value = jnp.exp2(s - top)
    e[part] = value
    m[j] = top
    l[j] = jnp.sum(value, axis=0, keepdims=True)


def block_state(m, l, state):
    tiles = m.shape[0]
    top = m[0]
    for j in range(1, tiles):
        top = jnp.maximum(top, m[j])
    total = l[0] * jnp.exp2(m[0] - top)
    for j in range(1, tiles):
        total += l[j] * jnp.exp2(m[j] - top)
    state[0:1] = top
    state[1:2] = total


def flat_positive(valid, positive):
    boxes = valid.shape[1]
    shape = (boxes, positive.shape[1])
    row = lax.broadcasted_iota(jnp.int32, shape, 0)
    spread = (row == lax.broadcasted_iota(jnp.int32, shape, 1) % boxes).astype(jnp.float32)
    wide = jnp.dot(
        valid[...].astype(jnp.float32), spread, preferred_element_type=jnp.float32
    )
    shape = wide.shape
    row = lax.broadcasted_iota(jnp.int32, shape, 0)
    image = lax.broadcasted_iota(jnp.int32, shape, 1) // boxes
    weight = jnp.sum(jnp.where(row == image, wide, 0.0), axis=0, keepdims=True)
    return jnp.where(weight > 0.5, positive[...], -1)


def first_scores_kernel(
    blk, p_hbm, r_hbm, pos_hbm, valid_hbm, e, m, state, phrases, regions, pos, l, pos_in, valid, sem
):
    tiles = m.shape[0]
    copies = [pltpu.make_async_copy(r_hbm, regions, sem.at[tiles])]
    for j in range(tiles):
        rows = pl.ds(pl.multiple_of(blk[j] * BLK, BLK), BLK)
        copies.append(
            pltpu.make_async_copy(p_hbm.at[rows], phrases.at[pl.ds(j * BLK, BLK)], sem.at[j])
        )
    small = [
        pltpu.make_async_copy(pos_hbm, pos_in, sem.at[tiles + 1]),
        pltpu.make_async_copy(valid_hbm, valid, sem.at[tiles + 2]),
    ]
    for copy in small + copies:
        copy.start()
    for copy in small:
        copy.wait()
    pos[...] = flat_positive(valid, pos_in)
    for copy in copies[:3]:
        copy.wait()
    for j in range(2):
        score_block(j, phrases, regions, e, m, l)
    for copy in copies[3:]:
        copy.wait()
    for j in range(2, tiles):
        score_block(j, phrases, regions, e, m, l)
    block_state(m, l, state)


def first_scores_call(blk, phrases, regions, positive, valid):
    rows, dim = regions.shape
    half = phrases.shape[0] // 2
    tiles = half // BLK
    arrays = (phrases, regions, positive[None], valid)
    return call(
        first_scores_kernel,
        [SCALAR] + [HBM] * 4,
        [
            ((half, rows), jnp.float32),
            ((tiles, 1, rows), jnp.float32),
            ((2, rows), jnp.float32),
            ((half, dim), phrases.dtype),
            ((rows, dim), regions.dtype),
            ((1, rows), jnp.int32),
        ],
        "first_scores",
        scratch_shapes=[
            pltpu.VMEM((tiles, 1, rows), jnp.float32),
            pltpu.VMEM((1, rows), jnp.int32),
            pltpu.VMEM(valid.shape, jnp.int32),
            pltpu.SemaphoreType.DMA((tiles + 3,)),
        ],
    )(blk, *[pltpu.with_memory_space_constraint(a, pltpu.HBM) for a in arrays])


def scores_kernel(phrases, regions, e, m, state, l):
    for j in range(m.shape[0]):
        score_block(j, phrases, regions, e, m, l)
    block_state(m, l, state)


def scores_call(phrases, regions):
    rows, dim = regions.shape
    half = phrases.shape[0]
    tiles = half // BLK
    return call(
        scores_kernel,
        [WHOLE] * 2,
        [
            ((half, rows), jnp.float32),
            ((tiles, 1, rows), jnp.float32),
            ((2, rows), jnp.float32),
        ],
        "scores",
        scratch_shapes=[pltpu.VMEM((tiles, 1, rows), jnp.float32)],
    )(vmem(phrases), vmem(regions))


def coefficients(e, scale, pos, first):
    column = first + lax.broadcasted_iota(jnp.int32, e.shape, 0)
    return (e * scale - (column == pos).astype(jnp.float32)).astype(jnp.bfloat16)


def phrase_kernel(base, off, eo, ep, so, sp, po, pp, ro, rp, send_a, send_b, keep_a, keep_b):
    half = ro.shape[1] // 2
    places = (
        (send_a, 1, send_b, 1),
        (send_a, 0, keep_b, 1),
        (keep_a, 1, send_b, 0),
        (keep_a, 0, keep_b, 0),
    )
    for step, (a, ia, b, ib) in enumerate(places):
        j = base + step
        part = pl.ds(j * BLK, BLK)
        co = coefficients(eo[part], so[j], po[...], off[j])
        cp = coefficients(ep[part], sp[j], pp[...], off[j])
        acc = jnp.dot(co, ro[...], preferred_element_type=jnp.float32)
        acc += jnp.dot(cp, rp[...], preferred_element_type=jnp.float32)
        acc = logit_scale * acc
        a[ia] = acc[:, :half].astype(a.dtype)
        b[ib] = acc[:, half:].astype(b.dtype)


def phrase_call(base, off, *arrays):
    rows, dim = arrays[-1].shape
    shape = (2, BLK, dim // 2)
    return call(
        lambda *refs: phrase_kernel(base, *refs),
        [SCALAR] + [WHOLE] * len(arrays),
        [(shape, jnp.bfloat16)] * 2 + [(shape, jnp.float32)] * 2,
        "phrase_part",
    )(off, *[vmem(a) for a in arrays])


def region_rows(i, off, e, s, pos, phrases):
    lanes = pl.ds(i, BLK)
    coeff = jnp.concatenate(
        [
            coefficients(e[pl.ds(j * BLK, BLK), lanes], s[j, :, lanes], pos[:, lanes], off[j])
            for j in range(s.shape[0])
        ],
        axis=0,
    )
    return logit_scale * lax.dot_general(
        coeff, phrases[...], (((0,), (0,)), ((), ())), preferred_element_type=jnp.float32
    )


def pair_region_kernel(phr, off, e, s, pos, phrases, out):
    for i in range(0, s.shape[2], BLK):
        acc = region_rows(i, off, e, s, pos, phrases)
        for q in range(8):
            out[phr[0] ^ q, pl.ds(i, BLK)] = acc[:, q * 128 : (q + 1) * 128]


def pair_region_call(phr, off, e, s, pos, phrases):
    arrays = (e, s, pos, phrases)
    return call(
        pair_region_kernel,
        [SCALAR] * 2 + [WHOLE] * len(arrays),
        [((8, s.shape[2], 128), jnp.float32)],
        "pair_region_part",
    )(phr, off, *[vmem(a) for a in arrays])[0]


def own_region_kernel(
    phr, off, e, s, pos, phrases, from_pair, send_a, send_b, next_a, next_b, keep, acc
):
    rows = s.shape[2]
    half = rows // 2
    for i in range(0, rows, BLK):
        acc[...] = region_rows(i, off, e, s, pos, phrases)
        here, there = pl.ds(i, BLK), pl.ds(i % half, BLK)
        for k in range(8):
            dy, dz = k // 4, k % 4
            cols = pl.ds(pl.multiple_of((phr[0] ^ k) * 128, 128), 128)
            value = acc[:, cols] + from_pair[k, here]
            if dz == 0:
                keep[dy, here] = value
            elif i < half and dz == 3:
                next_a[dy, there] = value
            elif i < half:
                send_a[dz - 1, dy, there] = value.astype(send_a.dtype)
            elif dz == 1:
                next_b[dy, there] = value
            else:
                send_b[3 - dz, dy, there] = value.astype(send_b.dtype)


def own_region_call(phr, off, e, s, pos, phrases, from_pair):
    rows = s.shape[2]
    half = rows // 2
    arrays = (e, s, pos, phrases, from_pair)
    return call(
        own_region_kernel,
        [SCALAR] * 2 + [WHOLE] * len(arrays),
        [((2, 2, half, 128), jnp.bfloat16)] * 2
        + [((2, half, 128), jnp.float32)] * 2
        + [((2, rows, 128), jnp.float32)],
        "own_region_part",
        scratch_shapes=[pltpu.VMEM((BLK, phrases.shape[1]), jnp.float32)],
    )(phr, off, *[vmem(a) for a in arrays])


def combine(first, second):
    top = jnp.maximum(first[0], second[0])
    total = first[1] * jnp.exp2(first[0] - top) + second[1] * jnp.exp2(second[0] - top)
    return jnp.stack([top, total])


def after(value, *others):
    return lax.optimization_barrier((value, *others))


def region_sum(send_a, send_b, next_a, next_b, keep):
    half = keep.shape[1] // 2
    got_a = over_phr(send_a, 0, 1).astype(jnp.float32)
    got_b = over_phr(send_b, 0, 3).astype(jnp.float32)
    last_a = over_phr((next_a + got_a[1]).astype(jnp.bfloat16), 0, 3).astype(jnp.float32)
    last_b = over_phr((next_b + got_b[1]).astype(jnp.bfloat16), 0, 1).astype(jnp.float32)
    total = jnp.concatenate(
        [keep[:, :half] + got_a[0] + last_a, keep[:, half:] + got_b[0] + last_b], axis=1
    )
    other = over_phr(total[1].astype(jnp.bfloat16), 1, 0).astype(jnp.float32)
    return (total[0] + other).astype(jnp.bfloat16)


def per_device(regions, phrases, positive, valid):
    img, phr = lax.axis_index("img"), lax.axis_index("phr")
    blk = jnp.stack([img ^ (e * 8 + d * 2) for e in (1, 0) for d in ORDER]).astype(jnp.int32)
    off = (phr * phrases.shape[0] + blk * BLK).astype(jnp.int32)
    blk, off, phr_id = after(blk, off, phr.astype(jnp.int32)[None])

    regions_pair = over_img(regions, CORE)
    e_own, m_own, own, phrases, regions, po = first_scores_call(
        blk, phrases, regions, positive, valid
    )
    pp = over_img(po, CORE)
    e_pair, m_pair, pair = scores_call(phrases, regions_pair)

    state = jnp.stack([own, pair], axis=1)
    state = combine(state, over_img(jnp.stack([pair, own], axis=1), CORE))
    for dy, dz in ((1, 0), (0, 1), (0, 3)):
        state = combine(state, over_phr(state, dy, dz))
    lse = state[0] + jnp.log2(state[1])
    s_own = jnp.where(po >= 0, jnp.exp2(m_own - lse[0]), 0.0)
    s_pair = jnp.where(pp >= 0, jnp.exp2(m_pair - lse[1]), 0.0)

    def phrase_half(base, off):
        return phrase_call(
            base, off, e_own, e_pair, s_own, s_pair, po, pp, regions, regions_pair
        )

    def first_step(send_a, send_b, keep_a, keep_b):
        sum_a = keep_a + over_img(send_a, X1).astype(jnp.float32)
        sum_b = keep_b + over_img(send_b, X3).astype(jnp.float32)
        return sum_a[0], sum_b[0], sum_a[1].astype(jnp.bfloat16), sum_b[1].astype(jnp.bfloat16)

    def second_step(sum_a, sum_b, send_a, send_b):
        last_a = over_img(send_a, X3).astype(jnp.float32)
        last_b = over_img(send_b, X1).astype(jnp.float32)
        return jnp.concatenate([sum_a + last_a, sum_b + last_b], axis=1)

    for_pair = pair_region_call(phr_id, off, e_pair, s_pair, pp, phrases)
    for_pair, off = after(for_pair, off)
    from_pair = over_img(for_pair, CORE)
    far = phrase_half(0, off)
    send_a, send_b, off = after(far[0], far[1], off)
    far = first_step(send_a, send_b, *far[2:])
    kept = own_region_call(phr_id, off, e_own, s_own, po, phrases, from_pair)
    send_a, send_b, off = after(kept[0], kept[1], off)
    grad_regions = region_sum(send_a, send_b, *kept[2:])
    near = phrase_half(4, off)
    near = first_step(*near)
    far = second_step(*far)
    near = second_step(*near)
    grad_phrases = near + over_img(far.astype(jnp.bfloat16), YH).astype(jnp.float32)
    return grad_regions, grad_phrases.astype(jnp.bfloat16)


def solution(mesh):
    in_specs = (P("img", None), P("phr", None), P("img"), P("img", None))
    out_specs = (P("img", "phr"), P(("phr", "img"), None))
    return jax.shard_map(
        per_device, mesh=mesh, in_specs=in_specs, out_specs=out_specs, check_vma=False
    )
```

```python
import math

import jax
import jax.numpy as jnp
from jax import lax
from jax.experimental import pallas as pl
from jax.experimental.pallas import tpu as pltpu
from jax.sharding import PartitionSpec as P

logit_scale = 2.0
log2e = math.log2(math.e)
BLK = 256
VMEM = 8 * 1024 * 1024


def img_perm(f):
    pairs = []
    for y in range(2):
        for x in range(4):
            for c in range(2):
                y2, x2, c2 = f(y, x, c)
                pairs.append(((y * 4 + x) * 2 + c, (y2 * 4 + x2) * 2 + c2))
    return pairs


def phr_perm(f):
    pairs = []
    for y in range(2):
        for z in range(4):
            y2, z2 = f(y, z)
            pairs.append((y * 4 + z, y2 * 4 + z2))
    return pairs


CORE = img_perm(lambda y, x, c: (y, x, 1 - c))
YH = img_perm(lambda y, x, c: (1 - y, x, c))
YL = phr_perm(lambda y, z: (1 - y, z))
NEAR = ((1, 3), (3, 1))
X = [img_perm(lambda y, x, c: (y, x ^ NEAR[step][c], c)) for step in range(2)]
Z = [
    [
        (i * 8 + p, i * 8 + q)
        for i in range(16)
        for p, q in phr_perm(lambda y, z: (y, z ^ NEAR[step][i % 2]))
    ]
    for step in range(2)
]


def over_img(a, perm):
    return lax.ppermute(a, "img", perm)


def over_phr(a, dy, dz):
    return lax.ppermute(a, "phr", phr_perm(lambda y, z: (y ^ dy, z ^ dz)))


def over_z(a, step):
    return lax.ppermute(a, ("img", "phr"), Z[step])


def vmem(a):
    return pltpu.with_memory_space_constraint(a, pltpu.VMEM)


WHOLE = pl.BlockSpec(memory_space=pltpu.VMEM)
SCALAR = pl.BlockSpec(memory_space=pltpu.SMEM)
HBM = pl.BlockSpec(memory_space=pltpu.HBM)


def call(body, in_specs, outs, name, waits=0, **kwargs):
    def kernel(*refs):
        body(*refs[: len(in_specs)], *refs[len(in_specs) + waits :])

    return pl.pallas_call(
        kernel,
        in_specs=in_specs + [pl.BlockSpec(memory_space=pl.ANY)] * waits,
        out_specs=[WHOLE] * len(outs),
        out_shape=[pltpu.VMEM(*out) for out in outs],
        compiler_params=pltpu.CompilerParams(vmem_limit_bytes=VMEM),
        cost_estimate=pl.CostEstimate(flops=1, bytes_accessed=1, transcendentals=0),
        name=name,
        **kwargs,
    )


def score_block(j, phrases, regions, e, m, l):
    part = pl.ds(j * BLK, BLK)
    s = lax.dot_general(
        phrases[part], regions[...], (((1,), (1,)), ((), ())), preferred_element_type=jnp.float32
    )
    s = s * (logit_scale * log2e)
    top = jnp.max(s, axis=0, keepdims=True)
    value = jnp.exp2(s - top)
    e[part] = value.astype(e.dtype)
    m[j] = top
    l[j] = jnp.sum(value, axis=0, keepdims=True)


def block_state(m, l, state, before=None):
    tiles = m.shape[0]
    top = m[0]
    for j in range(1, tiles):
        top = jnp.maximum(top, m[j])
    if before is not None:
        top = jnp.maximum(top, before[0:1])
    total = l[0] * jnp.exp2(m[0] - top)
    for j in range(1, tiles):
        total += l[j] * jnp.exp2(m[j] - top)
    if before is not None:
        total += before[1:2] * jnp.exp2(before[0:1] - top)
    state[0:1] = top
    state[1:2] = total


def flat_positive(valid, positive):
    boxes = valid.shape[1]
    shape = (boxes, positive.shape[1])
    row = lax.broadcasted_iota(jnp.int32, shape, 0)
    spread = (row == lax.broadcasted_iota(jnp.int32, shape, 1) % boxes).astype(jnp.float32)
    wide = jnp.dot(
        valid[...].astype(jnp.float32), spread, preferred_element_type=jnp.float32
    )
    shape = wide.shape
    row = lax.broadcasted_iota(jnp.int32, shape, 0)
    image = lax.broadcasted_iota(jnp.int32, shape, 1) // boxes
    weight = jnp.sum(jnp.where(row == image, wide, 0.0), axis=0, keepdims=True)
    return jnp.where(weight > 0.5, positive[...], -1)


def first_scores_kernel(blk, p_hbm, r_hbm, pos_hbm, valid_hbm, *refs):
    e, m, state, phrases, own, regions, pos, l, pos_in, valid, sem = refs
    tiles = m.shape[0]
    copies = [pltpu.make_async_copy(r_hbm, regions, sem.at[2 * tiles])]
    for out, start in ((phrases, tiles), (own, 0)):
        for j in range(tiles):
            rows = pl.ds(pl.multiple_of(blk[start + j] * BLK, BLK), BLK)
            copies.append(
                pltpu.make_async_copy(
                    p_hbm.at[rows], out.at[pl.ds(j * BLK, BLK)], sem.at[start + j]
                )
            )
    small = [
        pltpu.make_async_copy(pos_hbm, pos_in, sem.at[2 * tiles + 1]),
        pltpu.make_async_copy(valid_hbm, valid, sem.at[2 * tiles + 2]),
    ]
    for copy in small + copies[:3]:
        copy.start()
    for copy in small:
        copy.wait()
    pos[...] = flat_positive(valid, pos_in)
    for copy in copies[:3]:
        copy.wait()
    for copy in copies[3:]:
        copy.start()
    for j in range(2):
        score_block(j, phrases, regions, e, m, l)
    for copy in copies[3 : tiles + 1]:
        copy.wait()
    for j in range(2, tiles):
        score_block(j, phrases, regions, e, m, l)
    block_state(m, l, state)
    for copy in copies[tiles + 1 :]:
        copy.wait()


def first_scores_call(blk, phrases, regions, positive, valid):
    rows, dim = regions.shape
    half = phrases.shape[0] // 2
    tiles = half // BLK
    arrays = (phrases, regions, positive[None], valid)
    return call(
        first_scores_kernel,
        [SCALAR] + [HBM] * 4,
        [
            ((half, rows), jnp.bfloat16),
            ((tiles, 1, rows), jnp.float32),
            ((2, rows), jnp.float32),
            ((half, dim), phrases.dtype),
            ((half, dim), phrases.dtype),
            ((rows, dim), regions.dtype),
            ((1, rows), jnp.int32),
        ],
        "first_scores",
        scratch_shapes=[
            pltpu.VMEM((tiles, 1, rows), jnp.float32),
            pltpu.VMEM((1, rows), jnp.int32),
            pltpu.VMEM(valid.shape, jnp.int32),
            pltpu.SemaphoreType.DMA((2 * tiles + 3,)),
        ],
    )(blk, *[pltpu.with_memory_space_constraint(a, pltpu.HBM) for a in arrays])


def scores_kernel(phrases, regions, before, e, m, state, l):
    for j in range(m.shape[0]):
        score_block(j, phrases, regions, e, m, l)
    block_state(m, l, state, before)


def scores_call(phrases, regions, before):
    rows, dim = regions.shape
    half = phrases.shape[0]
    tiles = half // BLK
    arrays = (phrases, regions, before)
    return call(
        scores_kernel,
        [WHOLE] * len(arrays),
        [
            ((half, rows), jnp.float32),
            ((tiles, 1, rows), jnp.float32),
            ((2, rows), jnp.float32),
        ],
        "scores",
        scratch_shapes=[pltpu.VMEM((tiles, 1, rows), jnp.float32)],
    )(*[vmem(a) for a in arrays])


def coefficients(e, scale, pos, first):
    column = first + lax.broadcasted_iota(jnp.int32, e.shape, 0)
    return (e.astype(jnp.float32) * scale - (column == pos).astype(jnp.float32)).astype(jnp.bfloat16)


def phrase_kernel(base, off, eo, ep, so, sp, po, pp, ro, rp, send, keep):
    for step, (out, place) in enumerate(((send, 1), (send, 0), (keep, 1), (keep, 0))):
        j = base + step
        part = pl.ds(j * BLK, BLK)
        co = coefficients(eo[part], so[j], po[...], off[j])
        cp = coefficients(ep[part], sp[j], pp[...], off[j])
        acc = jnp.dot(co, ro[...], preferred_element_type=jnp.float32)
        acc += jnp.dot(cp, rp[...], preferred_element_type=jnp.float32)
        out[place] = (logit_scale * acc).astype(out.dtype)


def phrase_call(base, off, *arrays, wait):
    rows, dim = arrays[-1].shape
    shape = (2, BLK, dim)
    return call(
        lambda *refs: phrase_kernel(base, *refs),
        [SCALAR] + [WHOLE] * len(arrays),
        [(shape, jnp.bfloat16), (shape, jnp.float32)],
        "phrase_part",
        waits=len(wait),
    )(off, *[vmem(a) for a in arrays], *wait)


def add_kernel(got, keep, total, send):
    total[...] = keep[0] + got[0].astype(jnp.float32)
    send[...] = (keep[1] + got[1].astype(jnp.float32)).astype(send.dtype)


def add_call(got, keep, wait):
    shape = got.shape[1:]
    return call(
        add_kernel,
        [WHOLE] * 2,
        [(shape, jnp.float32), (shape, jnp.bfloat16)],
        "add_part",
        waits=len(wait),
    )(vmem(got), vmem(keep), *wait)


def region_rows(lanes, off, e, s, pos, phrases):
    coeff = jnp.concatenate(
        [
            coefficients(e[pl.ds(j * BLK, BLK), lanes], s[j, :, lanes], pos[:, lanes], off(j))
            for j in range(s.shape[0])
        ],
        axis=0,
    )
    return lax.dot_general(
        coeff, phrases[...], (((0,), (0,)), ((), ())), preferred_element_type=jnp.float32
    )


def region_kernel(phr, rel, off, e, s, phrases, e_far, s_far, p_far, pos, send, keep, acc):
    tiles = s.shape[0]
    for i in range(0, s.shape[2], BLK):
        here = pl.ds(i, BLK)
        value = region_rows(here, lambda j: off[j], e, s, pos, phrases)
        value += region_rows(here, lambda j: off[tiles + j], e_far, s_far, pos, p_far)
        acc[...] = logit_scale * value
        for dy in range(2):
            for place, (out, slot) in enumerate(((keep, 0), (send, 0), (send, 1), (keep, 1))):
                k = dy * 4 + rel[place]
                cols = pl.ds(pl.multiple_of((phr[0] ^ k) * 128, 128), 128)
                out[slot, dy, here] = acc[:, cols].astype(out.dtype)


def region_call(phr, rel, off, *arrays, wait):
    rows, dim = arrays[1].shape[2], arrays[2].shape[1]
    shape = (2, 2, rows, 128)
    return call(
        region_kernel,
        [SCALAR] * 3 + [WHOLE] * len(arrays),
        [(shape, jnp.bfloat16), (shape, jnp.float32)],
        "region_part",
        waits=len(wait),
        scratch_shapes=[pltpu.VMEM((BLK, dim), jnp.float32)],
    )(phr, rel, off, *[vmem(a) for a in arrays], *wait)


def combine(first, second):
    top = jnp.maximum(first[0], second[0])
    total = first[1] * jnp.exp2(first[0] - top) + second[1] * jnp.exp2(second[0] - top)
    return jnp.stack([top, total])


def per_device(regions, phrases, positive, valid):
    img, phr = lax.axis_index("img"), lax.axis_index("phr")
    core = img % 2
    first, second = 1 + 2 * core, 3 - 2 * core
    blk = jnp.stack(
        [img ^ (e * 8 + d * 2) for e in (1, 0) for d in (2, first, second, 0)]
        + [img ^ (e * 8 + d * 2 + 1) for e in (1, 0) for d in (2, second, first, 0)]
    )
    rel = jnp.stack([0 * core, first, 2 + 0 * core, second])
    off = phr * phrases.shape[0] + blk * BLK
    scalars = [a.astype(jnp.int32) for a in (blk, rel, off, phr[None])]
    blk, rel, off, phr = lax.optimization_barrier(scalars)

    regions_pair = over_img(regions, CORE)
    e_far, m_far, state, p_far, phrases, regions, po = first_scores_call(
        blk, phrases, regions, positive, valid
    )
    pp = over_img(po, CORE)
    e_pair = over_img(e_far, CORE)
    e_own, m_own, state = scores_call(phrases, regions, state)

    for dy, dz in ((1, 0), (0, 1), (0, 3)):
        state = combine(state, over_phr(state, dy, dz))
    lse = state[0] + jnp.log2(state[1])
    s_far = jnp.where(po >= 0, jnp.exp2(m_far - lse), 0.0)
    s_own = jnp.where(po >= 0, jnp.exp2(m_own - lse), 0.0)
    s_pair = over_img(s_far, CORE)

    def phrase_half(base, wait):
        return phrase_call(
            base, off, e_own, e_pair, s_own, s_pair, po, pp, regions, regions_pair, wait=wait
        )

    far_send, far_keep = phrase_half(0, [])
    far_got = over_img(far_send, X[0])
    send, keep = region_call(
        phr, rel, off, e_own, s_own, phrases, e_far, s_far, p_far, po, wait=[far_send]
    )
    got = over_z(send, 0)
    far_sum, far_send = add_call(far_got, far_keep, [send])
    near_send, near_keep = phrase_half(4, [far_send])
    near_got = over_img(near_send, X[0])
    far = far_sum + over_img(far_send, X[1]).astype(jnp.float32)
    far = far.astype(jnp.bfloat16)
    from_yh = over_img(far, YH)
    region_sum, send = add_call(got, keep, [far])
    region = region_sum + over_z(send, 1).astype(jnp.float32)
    send, from_yh = lax.optimization_barrier((region[1].astype(jnp.bfloat16), from_yh))
    from_yl = lax.ppermute(send, "phr", YL)
    near_sum, near_send = add_call(near_got, near_keep, [])
    near = near_sum + over_img(near_send, X[1]).astype(jnp.float32)
    grad_phrases = (near + from_yh.astype(jnp.float32)).astype(jnp.bfloat16)
    grad_regions = (region[0] + from_yl.astype(jnp.float32)).astype(jnp.bfloat16)
    return grad_regions, grad_phrases.astype(jnp.bfloat16)


def solution(mesh):
    in_specs = (P("img", None), P("phr", None), P("img"), P("img", None))
    out_specs = (P("img", "phr"), P(("phr", "img"), None))
    return jax.shard_map(
        per_device, mesh=mesh, in_specs=in_specs, out_specs=out_specs, check_vma=False
    )
```

```python
import math

import jax
import jax.numpy as jnp
from jax import lax
from jax.experimental import pallas as pl
from jax.experimental.pallas import tpu as pltpu
from jax.sharding import PartitionSpec as P

logit_scale = 2.0
log2e = math.log2(math.e)
BLK = 256
VMEM = 8 * 1024 * 1024


def img_perm(f):
    pairs = []
    for y in range(2):
        for x in range(4):
            for c in range(2):
                y2, x2, c2 = f(y, x, c)
                pairs.append(((y * 4 + x) * 2 + c, (y2 * 4 + x2) * 2 + c2))
    return pairs


def phr_perm(f):
    pairs = []
    for y in range(2):
        for z in range(4):
            y2, z2 = f(y, z)
            pairs.append((y * 4 + z, y2 * 4 + z2))
    return pairs


CORE = img_perm(lambda y, x, c: (y, x, 1 - c))
YH = img_perm(lambda y, x, c: (1 - y, x, c))
YL = phr_perm(lambda y, z: (1 - y, z))
NEAR = ((1, 3), (3, 1))
X = [img_perm(lambda y, x, c: (y, x ^ NEAR[step][c], c)) for step in range(2)]
Z = [
    [
        (i * 8 + p, i * 8 + q)
        for i in range(16)
        for p, q in phr_perm(lambda y, z: (y, z ^ NEAR[step][i % 2]))
    ]
    for step in range(2)
]


def over_img(a, perm):
    return lax.ppermute(a, "img", perm)


def over_phr(a, dy, dz):
    return lax.ppermute(a, "phr", phr_perm(lambda y, z: (y ^ dy, z ^ dz)))


def over_z(a, step):
    return lax.ppermute(a, ("img", "phr"), Z[step])


def vmem(a):
    return pltpu.with_memory_space_constraint(a, pltpu.VMEM)


WHOLE = pl.BlockSpec(memory_space=pltpu.VMEM)
SCALAR = pl.BlockSpec(memory_space=pltpu.SMEM)
HBM = pl.BlockSpec(memory_space=pltpu.HBM)


def call(body, in_specs, outs, name, waits=0, **kwargs):
    def kernel(*refs):
        body(*refs[: len(in_specs)], *refs[len(in_specs) + waits :])

    return pl.pallas_call(
        kernel,
        in_specs=in_specs + [pl.BlockSpec(memory_space=pl.ANY)] * waits,
        out_specs=[WHOLE] * len(outs),
        out_shape=[pltpu.VMEM(*out) for out in outs],
        compiler_params=pltpu.CompilerParams(vmem_limit_bytes=VMEM),
        cost_estimate=pl.CostEstimate(flops=1, bytes_accessed=1, transcendentals=0),
        name=name,
        **kwargs,
    )


def score_block(j, phrases, regions, e, m, l):
    part = pl.ds(j * BLK, BLK)
    s = lax.dot_general(
        phrases[part], regions[...], (((1,), (1,)), ((), ())), preferred_element_type=jnp.float32
    )
    s = s * (logit_scale * log2e)
    top = jnp.max(s, axis=0, keepdims=True)
    value = jnp.exp2(s - top)
    e[part] = value.astype(e.dtype)
    m[j] = top
    l[j] = jnp.sum(value, axis=0, keepdims=True)


def block_state(m, l, state, before=None):
    tiles = m.shape[0]
    top = m[0]
    for j in range(1, tiles):
        top = jnp.maximum(top, m[j])
    if before is not None:
        top = jnp.maximum(top, before[0:1])
    total = l[0] * jnp.exp2(m[0] - top)
    for j in range(1, tiles):
        total += l[j] * jnp.exp2(m[j] - top)
    if before is not None:
        total += before[1:2] * jnp.exp2(before[0:1] - top)
    state[0:1] = top
    state[1:2] = total


def flat_positive(valid, positive):
    boxes = valid.shape[1]
    shape = (boxes, positive.shape[1])
    row = lax.broadcasted_iota(jnp.int32, shape, 0)
    spread = (row == lax.broadcasted_iota(jnp.int32, shape, 1) % boxes).astype(jnp.float32)
    wide = jnp.dot(
        valid[...].astype(jnp.float32), spread, preferred_element_type=jnp.float32
    )
    shape = wide.shape
    row = lax.broadcasted_iota(jnp.int32, shape, 0)
    image = lax.broadcasted_iota(jnp.int32, shape, 1) // boxes
    weight = jnp.sum(jnp.where(row == image, wide, 0.0), axis=0, keepdims=True)
    return jnp.where(weight > 0.5, positive[...], -1)


def first_scores_kernel(blk, p_hbm, r_hbm, pos_hbm, valid_hbm, *refs):
    e, m, state, phrases, own, regions, pos, l, pos_in, valid, sem = refs
    tiles = m.shape[0]
    copies = [pltpu.make_async_copy(r_hbm, regions, sem.at[2 * tiles])]
    for out, start in ((phrases, tiles), (own, 0)):
        for j in range(tiles):
            rows = pl.ds(pl.multiple_of(blk[start + j] * BLK, BLK), BLK)
            copies.append(
                pltpu.make_async_copy(
                    p_hbm.at[rows], out.at[pl.ds(j * BLK, BLK)], sem.at[start + j]
                )
            )
    small = [
        pltpu.make_async_copy(pos_hbm, pos_in, sem.at[2 * tiles + 1]),
        pltpu.make_async_copy(valid_hbm, valid, sem.at[2 * tiles + 2]),
    ]
    for copy in small + copies[:3]:
        copy.start()
    for copy in small:
        copy.wait()
    pos[...] = flat_positive(valid, pos_in)
    for copy in copies[:3]:
        copy.wait()
    for copy in copies[3:]:
        copy.start()
    for j in range(2):
        score_block(j, phrases, regions, e, m, l)
    for copy in copies[3 : tiles + 1]:
        copy.wait()
    for j in range(2, tiles):
        score_block(j, phrases, regions, e, m, l)
    block_state(m, l, state)
    for copy in copies[tiles + 1 :]:
        copy.wait()


def first_scores_call(blk, phrases, regions, positive, valid):
    rows, dim = regions.shape
    half = phrases.shape[0] // 2
    tiles = half // BLK
    arrays = (phrases, regions, positive[None], valid)
    return call(
        first_scores_kernel,
        [SCALAR] + [HBM] * 4,
        [
            ((half, rows), jnp.bfloat16),
            ((tiles, 1, rows), jnp.float32),
            ((2, rows), jnp.float32),
            ((half, dim), phrases.dtype),
            ((half, dim), phrases.dtype),
            ((rows, dim), regions.dtype),
            ((1, rows), jnp.int32),
        ],
        "first_scores",
        scratch_shapes=[
            pltpu.VMEM((tiles, 1, rows), jnp.float32),
            pltpu.VMEM((1, rows), jnp.int32),
            pltpu.VMEM(valid.shape, jnp.int32),
            pltpu.SemaphoreType.DMA((2 * tiles + 3,)),
        ],
    )(blk, *[pltpu.with_memory_space_constraint(a, pltpu.HBM) for a in arrays])


def scores_kernel(phrases, regions, before, e, m, state, l):
    for j in range(m.shape[0]):
        score_block(j, phrases, regions, e, m, l)
    block_state(m, l, state, before)


def scores_call(phrases, regions, before):
    rows, dim = regions.shape
    half = phrases.shape[0]
    tiles = half // BLK
    arrays = (phrases, regions, before)
    return call(
        scores_kernel,
        [WHOLE] * len(arrays),
        [
            ((half, rows), jnp.float32),
            ((tiles, 1, rows), jnp.float32),
            ((2, rows), jnp.float32),
        ],
        "scores",
        scratch_shapes=[pltpu.VMEM((tiles, 1, rows), jnp.float32)],
    )(*[vmem(a) for a in arrays])


def coefficients(e, scale, pos, first):
    column = first + lax.broadcasted_iota(jnp.int32, e.shape, 0)
    return (e.astype(jnp.float32) * scale - (column == pos).astype(jnp.float32)).astype(jnp.bfloat16)


def phrase_kernel(base, off, eo, ep, so, sp, po, pp, ro, rp, out):
    for step in range(2):
        j = base + step
        part = pl.ds(j * BLK, BLK)
        co = coefficients(eo[part], so[j], po[...], off[j])
        cp = coefficients(ep[part], sp[j], pp[...], off[j])
        acc = jnp.dot(co, ro[...], preferred_element_type=jnp.float32)
        acc += jnp.dot(cp, rp[...], preferred_element_type=jnp.float32)
        out[1 - step] = (logit_scale * acc).astype(out.dtype)


def phrase_call(base, dtype, off, *arrays, wait):
    rows, dim = arrays[-1].shape
    return call(
        lambda *refs: phrase_kernel(base, *refs),
        [SCALAR] + [WHOLE] * len(arrays),
        [((2, BLK, dim), dtype)],
        "phrase_part",
        waits=len(wait),
    )(off, *[vmem(a) for a in arrays], *wait)[0]


def add_kernel(got, keep, total, send):
    total[...] = keep[0] + got[0].astype(jnp.float32)
    send[...] = (keep[1] + got[1].astype(jnp.float32)).astype(send.dtype)


def add_call(got, keep, wait):
    shape = got.shape[1:]
    return call(
        add_kernel,
        [WHOLE] * 2,
        [(shape, jnp.float32), (shape, jnp.bfloat16)],
        "add_part",
        waits=len(wait),
    )(vmem(got), vmem(keep), *wait)


def region_rows(lanes, off, e, s, pos, phrases):
    coeff = jnp.concatenate(
        [
            coefficients(e[pl.ds(j * BLK, BLK), lanes], s[j, :, lanes], pos[:, lanes], off(j))
            for j in range(s.shape[0])
        ],
        axis=0,
    )
    return lax.dot_general(
        coeff, phrases[...], (((0,), (0,)), ((), ())), preferred_element_type=jnp.float32
    )


def region_kernel(phr, rel, off, e, s, phrases, e_far, s_far, p_far, pos, send, keep, acc):
    tiles = s.shape[0]
    for i in range(0, s.shape[2], BLK):
        here = pl.ds(i, BLK)
        value = region_rows(here, lambda j: off[j], e, s, pos, phrases)
        value += region_rows(here, lambda j: off[tiles + j], e_far, s_far, pos, p_far)
        acc[...] = logit_scale * value
        for dy in range(2):
            for place, (out, slot) in enumerate(((keep, 0), (send, 0), (send, 1), (keep, 1))):
                k = dy * 4 + rel[place]
                cols = pl.ds(pl.multiple_of((phr[0] ^ k) * 128, 128), 128)
                out[slot, dy, here] = acc[:, cols].astype(out.dtype)


def region_call(phr, rel, off, *arrays, wait):
    rows, dim = arrays[1].shape[2], arrays[2].shape[1]
    shape = (2, 2, rows, 128)
    return call(
        region_kernel,
        [SCALAR] * 3 + [WHOLE] * len(arrays),
        [(shape, jnp.bfloat16), (shape, jnp.float32)],
        "region_part",
        waits=len(wait),
        scratch_shapes=[pltpu.VMEM((BLK, dim), jnp.float32)],
    )(phr, rel, off, *[vmem(a) for a in arrays], *wait)


def combine(first, second):
    top = jnp.maximum(first[0], second[0])
    total = first[1] * jnp.exp2(first[0] - top) + second[1] * jnp.exp2(second[0] - top)
    return jnp.stack([top, total])


def per_device(regions, phrases, positive, valid):
    img, phr = lax.axis_index("img"), lax.axis_index("phr")
    core = img % 2
    first, second = 1 + 2 * core, 3 - 2 * core
    blk = jnp.stack(
        [img ^ (e * 8 + d * 2) for e in (1, 0) for d in (2, first, second, 0)]
        + [img ^ (e * 8 + d * 2 + 1) for e in (1, 0) for d in (2, second, first, 0)]
    )
    rel = jnp.stack([0 * core, first, 2 + 0 * core, second])
    off = phr * phrases.shape[0] + blk * BLK
    scalars = [a.astype(jnp.int32) for a in (blk, rel, off, phr[None])]
    blk, rel, off, phr = lax.optimization_barrier(scalars)

    regions_pair = over_img(regions, CORE)
    e_far, m_far, state, p_far, phrases, regions, po = first_scores_call(
        blk, phrases, regions, positive, valid
    )
    pp = over_img(po, CORE)
    e_pair = over_img(e_far, CORE)
    e_own, m_own, state = scores_call(phrases, regions, state)

    for dy, dz in ((1, 0), (0, 1), (0, 3)):
        state = combine(state, over_phr(state, dy, dz))
    lse = state[0] + jnp.log2(state[1])
    s_far = jnp.where(po >= 0, jnp.exp2(m_far - lse), 0.0)
    s_own = jnp.where(po >= 0, jnp.exp2(m_own - lse), 0.0)
    s_pair = over_img(s_far, CORE)

    def phrases_of(base, dtype, wait):
        arrays = (e_own, e_pair, s_own, s_pair, po, pp, regions, regions_pair)
        return phrase_call(base, dtype, off, *arrays, wait=wait)

    far_send = phrases_of(0, jnp.bfloat16, [])
    far_got = over_img(far_send, X[0])
    far_keep = phrases_of(2, jnp.float32, [far_send])
    send, keep = region_call(
        phr, rel, off, e_own, s_own, phrases, e_far, s_far, p_far, po, wait=[far_keep]
    )
    got = over_z(send, 0)
    far_sum, far_send = add_call(far_got, far_keep, [send])
    near_send = phrases_of(4, jnp.bfloat16, [far_send])
    near_got = over_img(near_send, X[0])
    near_keep = phrases_of(6, jnp.float32, [near_send])
    far = far_sum + over_img(far_send, X[1]).astype(jnp.float32)
    far = far.astype(jnp.bfloat16)
    from_yh = over_img(far, YH)
    region_sum, send = add_call(got, keep, [far, near_keep])
    near_sum, near_send = add_call(near_got, near_keep, [])
    from_z, from_yh, near_sum = lax.optimization_barrier((over_z(send, 1), from_yh, near_sum))
    region = region_sum + from_z.astype(jnp.float32)
    from_yl = lax.ppermute(region[1].astype(jnp.bfloat16), "phr", YL)
    near = near_sum + over_img(near_send, X[1]).astype(jnp.float32)
    grad_phrases = (near + from_yh.astype(jnp.float32)).astype(jnp.bfloat16)
    from_yl, grad_phrases = lax.optimization_barrier((from_yl, grad_phrases))
    grad_regions = (region[0] + from_yl.astype(jnp.float32)).astype(jnp.bfloat16)
    return grad_regions, grad_phrases.astype(jnp.bfloat16)


def solution(mesh):
    in_specs = (P("img", None), P("phr", None), P("img"), P("img", None))
    out_specs = (P("img", "phr"), P(("phr", "img"), None))
    return jax.shard_map(
        per_device, mesh=mesh, in_specs=in_specs, out_specs=out_specs, check_vma=False
    )
```

```python
import math

import jax
import jax.numpy as jnp
from jax import lax
from jax.experimental import pallas as pl
from jax.experimental.pallas import tpu as pltpu
from jax.sharding import PartitionSpec as P

logit_scale = 2.0
log2e = math.log2(math.e)
BLK = 256
VMEM = 8 * 1024 * 1024


def img_perm(f):
    pairs = []
    for y in range(2):
        for x in range(4):
            for c in range(2):
                y2, x2, c2 = f(y, x, c)
                pairs.append(((y * 4 + x) * 2 + c, (y2 * 4 + x2) * 2 + c2))
    return pairs


def phr_perm(f):
    pairs = []
    for y in range(2):
        for z in range(4):
            y2, z2 = f(y, z)
            pairs.append((y * 4 + z, y2 * 4 + z2))
    return pairs


CORE = img_perm(lambda y, x, c: (y, x, 1 - c))
YH = img_perm(lambda y, x, c: (1 - y, x, c))
YL = phr_perm(lambda y, z: (1 - y, z))
NEAR = ((1, 3), (3, 1))
X = [img_perm(lambda y, x, c: (y, x ^ NEAR[step][c], c)) for step in range(2)]
Z = [
    [
        (i * 8 + p, i * 8 + q)
        for i in range(16)
        for p, q in phr_perm(lambda y, z: (y, z ^ NEAR[step][i % 2]))
    ]
    for step in range(2)
]


def over_img(a, perm):
    return lax.ppermute(a, "img", perm)


def over_phr(a, dy, dz):
    return lax.ppermute(a, "phr", phr_perm(lambda y, z: (y ^ dy, z ^ dz)))


def over_z(a, step):
    return lax.ppermute(a, ("img", "phr"), Z[step])


def vmem(a):
    return pltpu.with_memory_space_constraint(a, pltpu.VMEM)


WHOLE = pl.BlockSpec(memory_space=pltpu.VMEM)
SCALAR = pl.BlockSpec(memory_space=pltpu.SMEM)
HBM = pl.BlockSpec(memory_space=pltpu.HBM)


def call(body, in_specs, outs, name, waits=0, **kwargs):
    def kernel(*refs):
        body(*refs[: len(in_specs)], *refs[len(in_specs) + waits :])

    return pl.pallas_call(
        kernel,
        in_specs=in_specs + [pl.BlockSpec(memory_space=pl.ANY)] * waits,
        out_specs=[WHOLE] * len(outs),
        out_shape=[pltpu.VMEM(*out) for out in outs],
        compiler_params=pltpu.CompilerParams(vmem_limit_bytes=VMEM),
        cost_estimate=pl.CostEstimate(flops=1, bytes_accessed=1, transcendentals=0),
        name=name,
        **kwargs,
    )


def score_block(j, phrases, regions, e, m, l):
    part = pl.ds(j * BLK, BLK)
    s = lax.dot_general(
        phrases[part], regions[...], (((1,), (1,)), ((), ())), preferred_element_type=jnp.float32
    )
    s = s * (logit_scale * log2e)
    top = jnp.max(s, axis=0, keepdims=True)
    value = jnp.exp2(s - top)
    e[part] = value.astype(e.dtype)
    m[j] = top
    l[j] = jnp.sum(value, axis=0, keepdims=True)


def block_state(m, l, state, before=None):
    tiles = m.shape[0]
    top = m[0]
    for j in range(1, tiles):
        top = jnp.maximum(top, m[j])
    if before is not None:
        top = jnp.maximum(top, before[0:1])
    total = l[0] * jnp.exp2(m[0] - top)
    for j in range(1, tiles):
        total += l[j] * jnp.exp2(m[j] - top)
    if before is not None:
        total += before[1:2] * jnp.exp2(before[0:1] - top)
    state[0:1] = top
    state[1:2] = total


def flat_positive(valid, positive):
    boxes = valid.shape[1]
    shape = (boxes, positive.shape[1])
    row = lax.broadcasted_iota(jnp.int32, shape, 0)
    spread = (row == lax.broadcasted_iota(jnp.int32, shape, 1) % boxes).astype(jnp.float32)
    wide = jnp.dot(
        valid[...].astype(jnp.float32), spread, preferred_element_type=jnp.float32
    )
    shape = wide.shape
    row = lax.broadcasted_iota(jnp.int32, shape, 0)
    image = lax.broadcasted_iota(jnp.int32, shape, 1) // boxes
    weight = jnp.sum(jnp.where(row == image, wide, 0.0), axis=0, keepdims=True)
    return jnp.where(weight > 0.5, positive[...], -1)


def first_scores_kernel(blk, p_hbm, r_hbm, pos_hbm, valid_hbm, *refs):
    e, m, state, phrases, own, regions, pos, l, pos_in, valid, sem = refs
    tiles = m.shape[0]
    copies = [pltpu.make_async_copy(r_hbm, regions, sem.at[2 * tiles])]
    for out, start in ((phrases, tiles), (own, 0)):
        for j in range(tiles):
            rows = pl.ds(pl.multiple_of(blk[start + j] * BLK, BLK), BLK)
            copies.append(
                pltpu.make_async_copy(
                    p_hbm.at[rows], out.at[pl.ds(j * BLK, BLK)], sem.at[start + j]
                )
            )
    small = [
        pltpu.make_async_copy(pos_hbm, pos_in, sem.at[2 * tiles + 1]),
        pltpu.make_async_copy(valid_hbm, valid, sem.at[2 * tiles + 2]),
    ]
    for copy in small + copies[:3]:
        copy.start()
    for copy in small:
        copy.wait()
    pos[...] = flat_positive(valid, pos_in)
    for copy in copies[:3]:
        copy.wait()
    for copy in copies[3:]:
        copy.start()
    for j in range(2):
        score_block(j, phrases, regions, e, m, l)
    for copy in copies[3 : tiles + 1]:
        copy.wait()
    for j in range(2, tiles):
        score_block(j, phrases, regions, e, m, l)
    block_state(m, l, state)
    for copy in copies[tiles + 1 :]:
        copy.wait()


def first_scores_call(blk, phrases, regions, positive, valid):
    rows, dim = regions.shape
    half = phrases.shape[0] // 2
    tiles = half // BLK
    arrays = (phrases, regions, positive[None], valid)
    return call(
        first_scores_kernel,
        [SCALAR] + [HBM] * 4,
        [
            ((half, rows), jnp.bfloat16),
            ((tiles, 1, rows), jnp.float32),
            ((2, rows), jnp.float32),
            ((half, dim), phrases.dtype),
            ((half, dim), phrases.dtype),
            ((rows, dim), regions.dtype),
            ((1, rows), jnp.int32),
        ],
        "first_scores",
        scratch_shapes=[
            pltpu.VMEM((tiles, 1, rows), jnp.float32),
            pltpu.VMEM((1, rows), jnp.int32),
            pltpu.VMEM(valid.shape, jnp.int32),
            pltpu.SemaphoreType.DMA((2 * tiles + 3,)),
        ],
    )(blk, *[pltpu.with_memory_space_constraint(a, pltpu.HBM) for a in arrays])


def scores_kernel(phrases, regions, before, e, m, state, l):
    for j in range(m.shape[0]):
        score_block(j, phrases, regions, e, m, l)
    block_state(m, l, state, before)


def scores_call(phrases, regions, before):
    rows, dim = regions.shape
    half = phrases.shape[0]
    tiles = half // BLK
    arrays = (phrases, regions, before)
    return call(
        scores_kernel,
        [WHOLE] * len(arrays),
        [
            ((half, rows), jnp.float32),
            ((tiles, 1, rows), jnp.float32),
            ((2, rows), jnp.float32),
        ],
        "scores",
        scratch_shapes=[pltpu.VMEM((tiles, 1, rows), jnp.float32)],
    )(*[vmem(a) for a in arrays])


def coefficients(e, scale, pos, first):
    column = first + lax.broadcasted_iota(jnp.int32, e.shape, 0)
    return (e.astype(jnp.float32) * scale - (column == pos).astype(jnp.float32)).astype(jnp.bfloat16)


def phrase_kernel(base, off, eo, ep, so, sp, po, pp, ro, rp, out):
    for step in range(2):
        j = base + step
        part = pl.ds(j * BLK, BLK)
        co = coefficients(eo[part], so[j], po[...], off[j])
        cp = coefficients(ep[part], sp[j], pp[...], off[j])
        acc = jnp.dot(co, ro[...], preferred_element_type=jnp.float32)
        acc += jnp.dot(cp, rp[...], preferred_element_type=jnp.float32)
        out[1 - step] = (logit_scale * acc).astype(out.dtype)


def phrase_call(base, dtype, off, *arrays, wait):
    rows, dim = arrays[-1].shape
    return call(
        lambda *refs: phrase_kernel(base, *refs),
        [SCALAR] + [WHOLE] * len(arrays),
        [((2, BLK, dim), dtype)],
        "phrase_part",
        waits=len(wait),
    )(off, *[vmem(a) for a in arrays], *wait)[0]


def add_kernel(got, keep, total, send):
    total[...] = keep[0] + got[0].astype(jnp.float32)
    send[...] = (keep[1] + got[1].astype(jnp.float32)).astype(send.dtype)


def add_call(got, keep, wait):
    shape = got.shape[1:]
    return call(
        add_kernel,
        [WHOLE] * 2,
        [(shape, jnp.float32), (shape, jnp.bfloat16)],
        "add_part",
        waits=len(wait),
    )(vmem(got), vmem(keep), *wait)


def region_rows(lanes, off, e, s, pos, phrases):
    coeff = jnp.concatenate(
        [
            coefficients(e[pl.ds(j * BLK, BLK), lanes], s[j, :, lanes], pos[:, lanes], off(j))
            for j in range(s.shape[0])
        ],
        axis=0,
    )
    return lax.dot_general(
        coeff, phrases[...], (((0,), (0,)), ((), ())), preferred_element_type=jnp.float32
    )


def region_kernel(phr, rel, off, e, s, phrases, e_far, s_far, p_far, pos, send, keep, acc):
    tiles = s.shape[0]
    for i in range(0, s.shape[2], 2 * BLK):
        here = pl.ds(i, 2 * BLK)
        value = region_rows(here, lambda j: off[j], e, s, pos, phrases)
        value += region_rows(here, lambda j: off[tiles + j], e_far, s_far, pos, p_far)
        acc[...] = logit_scale * value
        for dy in range(2):
            for place, (out, slot) in enumerate(((keep, 0), (send, 0), (send, 1), (keep, 1))):
                k = dy * 4 + rel[place]
                cols = pl.ds(pl.multiple_of((phr[0] ^ k) * 128, 128), 128)
                out[slot, dy, here] = acc[:, cols].astype(out.dtype)


def region_call(phr, rel, off, *arrays, wait):
    rows, dim = arrays[1].shape[2], arrays[2].shape[1]
    shape = (2, 2, rows, 128)
    return call(
        region_kernel,
        [SCALAR] * 3 + [WHOLE] * len(arrays),
        [(shape, jnp.bfloat16), (shape, jnp.float32)],
        "region_part",
        waits=len(wait),
        scratch_shapes=[pltpu.VMEM((2 * BLK, dim), jnp.float32)],
    )(phr, rel, off, *[vmem(a) for a in arrays], *wait)


def combine(first, second):
    top = jnp.maximum(first[0], second[0])
    total = first[1] * jnp.exp2(first[0] - top) + second[1] * jnp.exp2(second[0] - top)
    return jnp.stack([top, total])


def per_device(regions, phrases, positive, valid):
    img, phr = lax.axis_index("img"), lax.axis_index("phr")
    core = img % 2
    first, second = 1 + 2 * core, 3 - 2 * core
    blk = jnp.stack(
        [img ^ (e * 8 + d * 2) for e in (1, 0) for d in (2, first, second, 0)]
        + [img ^ (e * 8 + d * 2 + 1) for e in (1, 0) for d in (2, second, first, 0)]
    )
    rel = jnp.stack([0 * core, first, 2 + 0 * core, second])
    off = phr * phrases.shape[0] + blk * BLK
    scalars = [a.astype(jnp.int32) for a in (blk, rel, off, phr[None])]
    blk, rel, off, phr = lax.optimization_barrier(scalars)

    regions_pair = over_img(regions, CORE)
    e_far, m_far, state, p_far, phrases, regions, po = first_scores_call(
        blk, phrases, regions, positive, valid
    )
    pp = over_img(po, CORE)
    e_pair = over_img(e_far, CORE)
    e_own, m_own, state = scores_call(phrases, regions, state)

    for dy, dz in ((1, 0), (0, 1)):
        state = combine(state, over_phr(state, dy, dz))
    state, pp = lax.optimization_barrier((state, pp))
    state = combine(state, over_phr(state, 0, 3))
    lse = state[0] + jnp.log2(state[1])
    s_far = jnp.where(po >= 0, jnp.exp2(m_far - lse), 0.0)
    s_own = jnp.where(po >= 0, jnp.exp2(m_own - lse), 0.0)
    s_pair = over_img(s_far, CORE)

    def phrases_of(base, dtype, wait):
        arrays = (e_own, e_pair, s_own, s_pair, po, pp, regions, regions_pair)
        return phrase_call(base, dtype, off, *arrays, wait=wait)

    far_send = phrases_of(0, jnp.bfloat16, [])
    far_got = over_img(far_send, X[0])
    far_keep = phrases_of(2, jnp.float32, [far_send])
    send, keep = region_call(
        phr, rel, off, e_own, s_own, phrases, e_far, s_far, p_far, po, wait=[far_keep]
    )
    got = over_z(send, 0)
    far_sum, far_send = add_call(far_got, far_keep, [send])
    near_send = phrases_of(4, jnp.bfloat16, [far_send])
    near_got = over_img(near_send, X[0])
    near_keep = phrases_of(6, jnp.float32, [near_send])
    far = far_sum + over_img(far_send, X[1]).astype(jnp.float32)
    far = far.astype(jnp.bfloat16)
    from_yh = over_img(far, YH)
    region_sum, send = add_call(got, keep, [far, near_keep])
    near_sum, near_send = add_call(near_got, near_keep, [])
    from_z, from_yh, near_sum = lax.optimization_barrier((over_z(send, 1), from_yh, near_sum))
    region = region_sum + from_z.astype(jnp.float32)
    from_yl = lax.ppermute(region[1].astype(jnp.bfloat16), "phr", YL)
    near = near_sum + over_img(near_send, X[1]).astype(jnp.float32)
    grad_phrases = (near + from_yh.astype(jnp.float32)).astype(jnp.bfloat16)
    from_yl, grad_phrases = lax.optimization_barrier((from_yl, grad_phrases))
    grad_regions = (region[0] + from_yl.astype(jnp.float32)).astype(jnp.bfloat16)
    return grad_regions, grad_phrases.astype(jnp.bfloat16)


def solution(mesh):
    in_specs = (P("img", None), P("phr", None), P("img"), P("img", None))
    out_specs = (P("img", "phr"), P(("phr", "img"), None))
    return jax.shard_map(
        per_device, mesh=mesh, in_specs=in_specs, out_specs=out_specs, check_vma=False
    )
```
